1024 devices in a mesh: ctx: 64 (over z, x_hi), head: 8 (over y, x_lo), fsdp: 2 (over core).
Axes of the slice: x: 4 (x_hi: 2, x_lo: 2; x = x_hi * 2 + x_lo), y: 4, z: 32, core: 2. Of those that a mesh axis runs over, the one named last changes fastest.
Arguments:
- query_rows: bfloat16 [65536, 6144], P(('ctx', 'head'), 'fsdp'), may hold values from -400 to 400
- key_rows: bfloat16 [65536, 6144], P(('ctx', 'head'), 'fsdp'), may hold values from -8 to 8
- value_rows: bfloat16 [65536, 4096], P(('ctx', 'head'), 'fsdp'), may hold values from -6 to 6
- query_weight: bfloat16 [1536, 6144], P(('ctx', 'fsdp'), 'head'), may hold values from -6 to 6
- key_weight: bfloat16 [512, 4096], P(('ctx', 'fsdp'), 'head'), may hold values from -6 to 6
Outputs:
- attended: bfloat16 [65536, 4096], P('ctx', ('fsdp', 'head'))
- clipped_query: bfloat16 [1536, 6144], P(('ctx', 'fsdp'), 'head')
- clipped_key: bfloat16 [512, 4096], P(('ctx', 'fsdp'), 'head')
The draws below stay inside these ranges and needn't reach their ends.
All inputs are finite; a program needn't handle non-finite values.
Results may differ from the reference program's by a relative error of at most 0.0033.
Values may be sent and summed in bfloat16 or wider, within the bound.
A program may use at most 64 MiB of HBM per device.

```python
import math
import jax
import jax.numpy as jnp
from jax import lax

H = 32
DNOPE = 128
DROPE = 64
DV = 128
QR = 1536
KVR = 512
BLK = 1024
DQK = 192
SEQ = 65536


def query_key_pair(key):
    folded = jax.random.fold_in(key, 31)
    subkeys = jax.random.split(folded, 9)
    blocks = SEQ // BLK
    queries = 2.0 * jax.random.normal(subkeys[1], (SEQ, H, DQK), jnp.float32)
    keys_all = jax.random.normal(subkeys[2], (SEQ, H, DQK), jnp.float32)
    hot_slot = BLK // 2 + jax.random.randint(subkeys[3], (blocks, H), 0, BLK // 2)
    key_gap = jax.random.randint(subkeys[4], (blocks, H), 1, BLK // 4 + 1)
    strong = (jax.random.permutation(subkeys[5], H) < H // 2)[None, :]
    order = jax.random.permutation(subkeys[6], blocks)
    top_block = order[jnp.arange(H) % blocks]
    is_top = jnp.arange(blocks)[:, None] == top_block[None, :]
    levels = jax.random.uniform(subkeys[7], (blocks, H), jnp.float32)
    lower_bound = jnp.where(is_top, jnp.where(strong, 220.0, 60.0), jnp.where(strong, 40.0, 30.0))
    upper_bound = jnp.where(is_top, jnp.where(strong, 260.0, 95.0), jnp.where(strong, 140.0, 55.0))
    strength = lower_bound + (upper_bound - lower_bound) * levels
    spread = jax.random.uniform(subkeys[8], (blocks, H), jnp.float32, 1.0, 3.0)
    starts = (jnp.arange(blocks, dtype=jnp.int32) * BLK)[:, None]
    query_at = starts + hot_slot
    key_at = query_at - key_gap
    twin_at = key_at - 1
    head_ids = jnp.broadcast_to(jnp.arange(H, dtype=jnp.int32)[None, :], (blocks, H))
    target = keys_all[key_at, head_ids]
    norm_sq = jnp.sum(target * target, axis=-1, keepdims=True)
    keys_all = keys_all.at[twin_at, head_ids].set(target * (1.0 - spread / strength)[:, :, None])
    queries = queries.at[query_at, head_ids].set(target * (strength * math.sqrt(DQK))[:, :, None] / norm_sq)
    return (queries.reshape(SEQ, H * DQK), keys_all.reshape(SEQ, H * DQK))


def draw_query_rows(key, part):
    return query_key_pair(key)[0].astype(jnp.bfloat16)


def draw_key_rows(key, part):
    return query_key_pair(key)[1].astype(jnp.bfloat16)


def block_scale(key, shape, shards, least, high):
    def one(axis_at, blocks):
        steps = jax.random.uniform(jax.random.fold_in(jax.random.fold_in(key, 6), axis_at), (blocks,), jnp.float32, least / len(shards), high / len(shards))
        return jnp.repeat(jnp.exp(steps), shape[axis_at] // blocks).reshape((-1,) + (1,) * (len(shape) - axis_at - 1))

    level = one(*shards[0])
    for cut in shards[1:]:
        level = level * one(*cut)
    return level


def scatter_about(stream_key, shape, scale, most, cuts=(), kind=jnp.bfloat16):
    result = jax.random.normal(stream_key, shape, jnp.float32) * scale
    if len(cuts) > 0:
        result = block_scale(stream_key, shape, cuts, -0.22, 0.18) * result
    return jnp.clip(result, min=-most, max=most).astype(kind)


def setup_inputs(seed: int = 0) -> dict:
    streams_of = jax.random.split(jax.random.key(seed), 6)
    query_rows = draw_query_rows(jax.random.fold_in(streams_of[5], 71), 0)
    key_rows = draw_key_rows(jax.random.fold_in(streams_of[5], 71), 0)
    value_rows = scatter_about(streams_of[2], (SEQ, H * DV), 1.0, 6.0, ((0, 512), (1, 2)))
    query_weight = scatter_about(streams_of[3], (QR, H * DQK), 1.0, 6.0, ((0, 128), (1, 8)))
    key_weight = scatter_about(streams_of[4], (KVR, H * DNOPE), 1.0, 6.0, ((0, 128), (1, 8)))
    return {"query_rows": query_rows, "key_rows": key_rows, "value_rows": value_rows, "query_weight": query_weight, "key_weight": key_weight}


clip_threshold = 100.0

def partial_softmax(scores, value_block):
    highest = lax.optimization_barrier(jnp.max(scores, axis=2))
    present = jnp.isfinite(highest)
    shifted = jnp.where(present, highest, 0.0)
    weights = jnp.exp(scores - shifted[:, :, None])
    totals = lax.optimization_barrier(jnp.sum(weights, axis=2))
    rounded = lax.optimization_barrier(weights.astype(jnp.bfloat16))
    summed = jnp.einsum('htu,uhd->thd', rounded.astype(jnp.float32), value_block.astype(jnp.float32), precision=lax.Precision.HIGHEST)
    return (summed, totals, jnp.where(present, highest, -jnp.inf))

def merge_parts(own_part, far_part):
    own_sum, own_total, own_high = own_part
    far_sum, far_total, far_high = far_part
    highest = jnp.maximum(own_high, far_high)
    own_scale = jnp.exp(own_high - highest)
    far_scale = jnp.exp(far_high - highest)
    totals = own_total * own_scale + far_total * far_scale
    mixed = own_sum * own_scale.T[:, :, None] + far_sum * far_scale.T[:, :, None]
    return mixed / totals.T[:, :, None]

def take_block(source, first_row, width):
    return lax.dynamic_slice_in_dim(source, first_row, BLK, 0).reshape(BLK, H, width).astype(jnp.float32)

def head_scores(query_cube, key_cube):
    return jnp.einsum('thd,uhd->htu', query_cube, key_cube, precision=lax.Precision.HIGHEST) * DQK ** (-0.5)

def block_attention(block_index, query_rows, key_rows, value_rows):
    first_row = block_index * BLK
    before = jnp.maximum(first_row - BLK, 0)
    query_cube = take_block(query_rows, first_row, DQK)
    key_cube = take_block(key_rows, first_row, DQK)
    value_cube = take_block(value_rows, first_row, DV)
    far_key = take_block(key_rows, before, DQK)
    far_value = take_block(value_rows, before, DV)
    row_ids = lax.broadcasted_iota(jnp.int32, (BLK, BLK), 0)
    col_ids = lax.broadcasted_iota(jnp.int32, (BLK, BLK), 1)
    own_scores = jnp.where((row_ids >= col_ids)[None], head_scores(query_cube, key_cube), -jnp.inf)
    far_scores = jnp.where(block_index > 0, head_scores(query_cube, far_key), -jnp.inf)
    head_peak = jnp.maximum(lax.optimization_barrier(jnp.max(own_scores, axis=(1, 2))), lax.optimization_barrier(jnp.max(far_scores, axis=(1, 2))))
    mixed = merge_parts(partial_softmax(own_scores, value_cube), partial_softmax(far_scores, far_value))
    return (mixed.astype(jnp.bfloat16).reshape(BLK, H * DV), head_peak)

def reference(query_rows, key_rows, value_rows, query_weight, key_weight):
    block_ids = jnp.arange(SEQ // BLK, dtype=jnp.int32)
    attended, peaks = lax.map(lambda index_now: block_attention(index_now, query_rows, key_rows, value_rows), block_ids)
    attended = attended.reshape(SEQ, H * DV)
    head_peak = lax.optimization_barrier(jnp.max(peaks, axis=0))
    factor = jnp.minimum(1.0, clip_threshold / head_peak)
    root_factor = jnp.sqrt(factor)
    column_factor = jnp.concatenate([jnp.broadcast_to(root_factor[:, None], (H, DNOPE)), jnp.broadcast_to(factor[:, None], (H, DROPE))], axis=1)
    clipped_query = (query_weight.astype(jnp.float32).reshape(QR, H, DQK) * column_factor[None]).astype(jnp.bfloat16).reshape(QR, H * DQK)
    clipped_key = (key_weight.astype(jnp.float32).reshape(KVR, H, DNOPE) * root_factor[None, :, None]).astype(jnp.bfloat16).reshape(KVR, H * DNOPE)
    return (attended, clipped_query, clipped_key)
```

```python
import functools
import math

import jax
import jax.numpy as jnp
from jax import lax
from jax.experimental import pallas as pl
from jax.experimental.pallas import tpu as pltpu
from jax.sharding import PartitionSpec as P

DNOPE = 128
DROPE = 64
DV = 128
DQK = 192
HEADS = 2
CLIP = 100.0
SCALE = DQK**-0.5
ROWS = 128
BLK = 1024
TILE = 256
GROUP = 8
MESH = pl.DeviceIdType.MESH
WIDTH = (HEADS * DQK, HEADS * DQK, HEADS * DV)
FAR_ORDER = ((2, 1), (2, 0), (1, 1), (3, 1), (1, 0), (3, 0), (0, 1), (0, 0))


def attention_kernel(
    q_ref,
    k_ref,
    v_ref,
    wq_ref,
    wk_ref,
    out_ref,
    cq_ref,
    ck_ref,
    q_buf,
    k_buf,
    v_buf,
    p_buf,
    acc_buf,
    ones_buf,
    mine_buf,
    near_buf,
    group_buf,
    wide_buf,
    local_sem,
    own_send,
    own_recv,
    far_send,
    far_recv,
    near_send,
    near_recv,
    wide_send,
    wide_recv,
):
    ctx = lax.axis_index("ctx")
    head = lax.axis_index("head")
    core = lax.axis_index("fsdp")
    ctx_count = lax.axis_size("ctx")
    y, x = head // 2, head % 2
    group, member = ctx // GROUP, ctx % GROUP
    groups = ctx_count // GROUP
    owner_core, owner_base = head // 4, 2 * (head % 4)
    target_head = 4 * core + head // 2
    parity = head % 2
    is_own_target = target_head == head

    def peer(dy, dx):
        return lax.rem(y + dy, 4) * 2 + lax.rem(x + dx, 2)

    def place(to_ctx, to_head, to_core):
        return {"ctx": to_ctx, "head": to_head, "fsdp": to_core}

    def near_ctx(step):
        return group * GROUP + lax.rem(member + step, GROUP)

    def wide_ctx(step):
        return lax.rem(group + step, groups) * GROUP + member

    barrier = pltpu.get_barrier_semaphore()

    def greet(where):
        pl.semaphore_signal(barrier, inc=1, device_id=where, device_id_type=MESH)

    for dy, dx in FAR_ORDER[:-1]:
        greet(place(ctx, peer(dy, dx), core))

    @pl.when(ctx > 0)
    def _():
        for dy, dx in FAR_ORDER:
            greet(place(ctx - 1, peer(dy, dx), core))

    for step in range(1, GROUP):
        greet(place(near_ctx(step), head, core))
    for step in range(1, groups):
        for par in range(2):
            greet(place(wide_ctx(step), owner_base + par, owner_core))
    for par in range(2):

        @pl.when(jnp.logical_not((owner_base + par == head) & (owner_core == core)))
        def _():
            greet(place(ctx, owner_base + par, owner_core))

    pl.semaphore_wait(
        barrier,
        7
        + (GROUP - 1)
        + 2 * groups
        + jnp.where(ctx < ctx_count - 1, 8, 0)
        - jnp.where(is_own_target, 1, 0),
    )

    ins = (q_ref, k_ref, v_ref)
    bufs = (q_buf, k_buf, v_buf)

    def columns(ref, t, where):
        return ref.at[:, pl.ds(pl.multiple_of(where * WIDTH[t], 128), WIDTH[t])]

    def landing(t, offset):
        return bufs[t].at[pl.ds(pl.multiple_of(offset + head * ROWS, ROWS), ROWS), :]

    def own_copy(t, n):
        to = peer(*FAR_ORDER[n])
        return pltpu.make_async_remote_copy(
            src_ref=columns(ins[t], t, to),
            dst_ref=landing(t, 0),
            send_sem=own_send.at[t, n],
            recv_sem=own_recv.at[t, n],
            device_id=place(ctx, to, core),
            device_id_type=MESH,
        )

    def far_copy(t, n):
        to = peer(*FAR_ORDER[n])
        return pltpu.make_async_remote_copy(
            src_ref=columns(ins[t], t, to),
            dst_ref=landing(t, BLK),
            send_sem=far_send.at[t - 1, n],
            recv_sem=far_recv.at[t - 1, n],
            device_id=place(ctx + 1, to, core),
            device_id_type=MESH,
        )

    def local_copy(t):
        return pltpu.make_async_copy(columns(ins[t], t, head), landing(t, 0), local_sem.at[t])

    def start_own(t):
        for n in range(7):
            own_copy(t, n).start()
        local_copy(t).start()

    def start_far(t):
        @pl.when(ctx < ctx_count - 1)
        def _():
            for n in range(8):
                far_copy(t, n).start()

    def wait_own(t):
        local_copy(t).wait()
        for n in range(7):
            own_copy(t, n).wait_recv()

    def wait_far(t):
        @pl.when(ctx > 0)
        def _():
            for n in range(8):
                far_copy(t, n).wait_recv()

    start_own(0)
    start_own(1)
    start_far(1)
    start_own(2)
    start_far(2)

    ones_buf[...] = jnp.where(ctx > 0, 1.0, 0.0) * jnp.ones(ones_buf.shape, jnp.bfloat16)

    wait_own(0)
    wait_own(1)
    wait_far(1)

    @pl.when(ctx == 0)
    def _():
        k_buf[BLK:, :] = jnp.broadcast_to(k_buf[0:1, :], (BLK, WIDTH[1]))

    lanes = lax.broadcasted_iota(jnp.int32, (TILE, 2 * 128), 1)
    later = lax.broadcasted_iota(jnp.int32, (TILE, TILE), 0) < lax.broadcasted_iota(
        jnp.int32, (TILE, TILE), 1
    )
    contract = (((1,), (1,)), ((), ()))

    @pl.loop(0, HEADS)
    def _(h):
        window = pl.ds(pl.multiple_of(h * 128, 128), 256)
        valid = (lanes >= DROPE * h) & (lanes < DQK + DROPE * h)
        peak = jnp.full((1, 1), -jnp.inf, jnp.float32)
        for i in range(BLK // TILE):
            rows = slice(i * TILE, (i + 1) * TILE)
            query = jnp.where(valid, q_buf[rows, window], jnp.zeros((), jnp.bfloat16))
            parts = []
            if i > 0:
                parts.append(
                    lax.dot_general(
                        query, k_buf[: i * TILE, window], contract,
                        preferred_element_type=jnp.float32,
                    )
                )
            diagonal = lax.dot_general(
                query, k_buf[rows, window], contract, preferred_element_type=jnp.float32
            )
            parts.append(jnp.where(later, -jnp.inf, diagonal))
            parts.append(
                lax.dot_general(
                    query, k_buf[BLK:, window], contract, preferred_element_type=jnp.float32
                )
            )
            high = functools.reduce(
                jnp.maximum, [jnp.max(part, axis=1, keepdims=True) for part in parts]
            )
            starts = ([0] if i > 0 else []) + [i * TILE, BLK]
            for start, part in zip(starts, parts):
                weights = jnp.exp2((part - high) * (SCALE * math.log2(math.e)))
                p_buf[h, rows, start : start + part.shape[1]] = weights.astype(jnp.bfloat16)
            peak = jnp.maximum(peak, jnp.max(high, axis=0, keepdims=True))
        mine_buf[pl.ds(h, 1), :] = jnp.broadcast_to(peak * SCALE, (1, 128))

    def near_copy(step):
        return pltpu.make_async_remote_copy(
            src_ref=mine_buf,
            dst_ref=near_buf.at[step - 1],
            send_sem=near_send.at[step - 1],
            recv_sem=near_recv.at[step - 1],
            device_id=place(near_ctx(step), head, core),
            device_id_type=MESH,
        )

    for step in range(1, GROUP):
        near_copy(step).start()

    wait_own(2)

    def values(rows, h):
        return v_buf[rows, pl.ds(pl.multiple_of(h * 128, 128), DV)]

    @pl.loop(0, HEADS)
    def _(h):
        for i in range(BLK // TILE):
            rows = slice(i * TILE, (i + 1) * TILE)
            own = slice(0, (i + 1) * TILE)
            right = jnp.concatenate(
                [values(own, h), jnp.ones(((i + 1) * TILE, 128), jnp.bfloat16)], axis=1
            )
            acc_buf[h, rows, :] = jnp.dot(
                p_buf[h, rows, own], right, preferred_element_type=jnp.float32
            )

    for step in range(1, GROUP):
        near_copy(step).wait_recv()
    group_buf[...] = jnp.maximum(mine_buf[...], jnp.max(near_buf[...], axis=0))

    def wide_copy(step, dc):
        return pltpu.make_async_remote_copy(
            src_ref=group_buf,
            dst_ref=wide_buf.at[parity * GROUP + step],
            send_sem=wide_send.at[step, dc],
            recv_sem=wide_recv.at[parity * GROUP + step],
            device_id=place(wide_ctx(step), target_head, lax.rem(core + dc, 2)),
            device_id_type=MESH,
        )

    def wide_arrival(par, step):
        return pltpu.make_async_remote_copy(
            src_ref=group_buf,
            dst_ref=wide_buf.at[par * GROUP + step],
            send_sem=wide_send.at[step, 0],
            recv_sem=wide_recv.at[par * GROUP + step],
            device_id=place(wide_ctx(step), target_head, core),
            device_id_type=MESH,
        )

    for step in range(groups):
        for dc in range(2):
            if step == 0 and dc == 0:

                @pl.when(jnp.logical_not(is_own_target))
                def _():
                    wide_copy(0, 0).start()

                @pl.when(is_own_target)
                def _():
                    wide_buf[pl.ds(parity * GROUP, 1)] = group_buf[...][None]

            else:
                wide_copy(step, dc).start()

    wait_far(2)

    @pl.when(ctx == 0)
    def _():
        v_buf[BLK:, :] = jnp.zeros((BLK, WIDTH[2]), jnp.bfloat16)

    @pl.loop(0, HEADS)
    def _(h):
        right = jnp.concatenate([values(slice(BLK, 2 * BLK), h), ones_buf[...]], axis=1)
        for i in range(BLK // TILE):
            rows = slice(i * TILE, (i + 1) * TILE)
            total = acc_buf[h, rows, :] + jnp.dot(
                p_buf[h, rows, BLK:], right, preferred_element_type=jnp.float32
            )
            out_ref[rows, pl.ds(pl.multiple_of(h * 128, 128), DV)] = (
                total[:, :DV] / total[:, DV:]
            ).astype(jnp.bfloat16)

    for par in range(2):
        for step in range(groups):
            if step == 0:

                @pl.when(
                    jnp.logical_not((owner_base + par == head) & (owner_core == core))
                )
                def _():
                    wide_arrival(par, 0).wait_recv()

            else:
                wide_arrival(par, step).wait_recv()

    half = lax.broadcasted_iota(jnp.int32, (1, 128), 1) < DROPE
    for par in range(2):
        peaks = jnp.max(wide_buf[par * GROUP : (par + 1) * GROUP], axis=0)
        factors = jnp.minimum(1.0, CLIP / peaks)
        roots = jnp.sqrt(factors)
        first, second = factors[0:1], factors[1:2]
        root_first, root_second = roots[0:1], roots[1:2]
        tiles = (
            root_first,
            jnp.where(half, first, root_second),
            jnp.where(half, root_second, second),
        )
        for n, tile in enumerate(tiles):
            at = slice((par * 3 + n) * 128, (par * 3 + n + 1) * 128)
            cq_ref[:, at] = (wq_ref[:, at].astype(jnp.float32) * tile).astype(jnp.bfloat16)
        for n, tile in enumerate((root_first, root_second)):
            at = slice((par * 2 + n) * 128, (par * 2 + n + 1) * 128)
            ck_ref[:, at] = (wk_ref[:, at].astype(jnp.float32) * tile).astype(jnp.bfloat16)

    for t in range(3):
        for n in range(7):
            own_copy(t, n).wait_send()

    @pl.when(ctx < ctx_count - 1)
    def _():
        for t in (1, 2):
            for n in range(8):
                far_copy(t, n).wait_send()

    for step in range(1, GROUP):
        near_copy(step).wait_send()
    for step in range(groups):
        for dc in range(2):
            if step == 0 and dc == 0:

                @pl.when(jnp.logical_not(is_own_target))
                def _():
                    wide_copy(0, 0).wait_send()

            else:
                wide_copy(step, dc).wait_send()


def body(query_rows, key_rows, value_rows, query_weight, key_weight):
    vmem = pl.BlockSpec(memory_space=pltpu.VMEM)
    hbm = pl.BlockSpec(memory_space=pl.ANY)
    groups = lax.axis_size("ctx") // GROUP
    dma = pltpu.SemaphoreType.DMA
    return pl.pallas_call(
        attention_kernel,
        out_shape=(
            jax.ShapeDtypeStruct((BLK, HEADS * DV), jnp.bfloat16),
            jax.ShapeDtypeStruct(query_weight.shape, jnp.bfloat16),
            jax.ShapeDtypeStruct(key_weight.shape, jnp.bfloat16),
        ),
        in_specs=[hbm, hbm, hbm, vmem, vmem],
        out_specs=(vmem, vmem, vmem),
        scratch_shapes=[
            pltpu.VMEM((BLK, WIDTH[0]), jnp.bfloat16),
            pltpu.VMEM((2 * BLK, WIDTH[1]), jnp.bfloat16),
            pltpu.VMEM((2 * BLK, WIDTH[2]), jnp.bfloat16),
            pltpu.VMEM((HEADS, BLK, 2 * BLK), jnp.bfloat16),
            pltpu.VMEM((HEADS, BLK, 2 * DV), jnp.float32),
            pltpu.VMEM((BLK, 128), jnp.bfloat16),
            pltpu.VMEM((HEADS, 128), jnp.float32),
            pltpu.VMEM((GROUP - 1, HEADS, 128), jnp.float32),
            pltpu.VMEM((HEADS, 128), jnp.float32),
            pltpu.VMEM((2 * GROUP, HEADS, 128), jnp.float32),
            dma((3,)),
            dma((3, 7)),
            dma((3, 7)),
            dma((2, 8)),
            dma((2, 8)),
            dma((GROUP - 1,)),
            dma((GROUP - 1,)),
            dma((groups, 2)),
            dma((2 * GROUP,)),
        ],
        compiler_params=pltpu.CompilerParams(
            collective_id=0, has_side_effects=True, vmem_limit_bytes=56 * 1024 * 1024
        ),
        cost_estimate=pl.CostEstimate(
            flops=3_500_000_000, bytes_accessed=3_000_000, transcendentals=3_500_000
        ),
        name="attention",
    )(query_rows, key_rows, value_rows, query_weight, key_weight)


def solution(mesh):
    rows = P(("ctx", "head"), "fsdp")
    weights = P(("ctx", "fsdp"), "head")
    return jax.shard_map(
        body,
        mesh=mesh,
        in_specs=(rows, rows, rows, weights, weights),
        out_specs=(P("ctx", ("fsdp", "head")), weights, weights),
        check_vma=False,
    )
```

```python
import functools
import math

import jax
import jax.numpy as jnp
from jax import lax
from jax.experimental import pallas as pl
from jax.experimental.pallas import tpu as pltpu
from jax.sharding import PartitionSpec as P

DNOPE = 128
DROPE = 64
DV = 128
DQK = 192
HEADS = 2
CLIP = 100.0
SCALE = DQK**-0.5
ROWS = 128
BLK = 1024
TILE = 256
GROUP = 4
HEARD = (1, 2, 4, 8, 16)
MESH = pl.DeviceIdType.MESH
WIDTH = (HEADS * DQK, HEADS * DQK, HEADS * DV)
PEERS = ((2, 1), (2, 0), (1, 1), (3, 1), (1, 0), (3, 0), (0, 1), (0, 0))


def attention_kernel(
    q_ref,
    k_ref,
    v_ref,
    out_ref,
    peak_ref,
    q_buf,
    k_buf,
    v_buf,
    p_buf,
    acc_buf,
    high_buf,
    both_buf,
    far_buf,
    ones_buf,
    mine_buf,
    near_buf,
    part_buf,
    wide_buf,
    local_sem,
    own_send,
    own_recv,
    far_send,
    far_recv,
    near_send,
    near_recv,
    wide_send,
    wide_recv,
    known_sem,
):
    ctx = lax.axis_index("ctx")
    head = lax.axis_index("head")
    core = lax.axis_index("fsdp")
    ctx_count = lax.axis_size("ctx")
    y, x = head // 2, head % 2
    group, member = ctx // GROUP, ctx % GROUP
    groups = ctx_count // GROUP
    owner_core, owner_base = head // 4, 2 * (head % 4)
    target_head = 4 * core + head // 2
    parity = head % 2
    is_own_target = target_head == head

    def peer(dy, dx):
        return lax.rem(y + dy, 4) * 2 + lax.rem(x + dx, 2)

    def place(to_ctx, to_head, to_core):
        return {"ctx": to_ctx, "head": to_head, "fsdp": to_core}

    def ring(step):
        return lax.rem(ctx + step + ctx_count, ctx_count)

    barrier = pltpu.get_barrier_semaphore()

    def greet(where):
        pl.semaphore_signal(barrier, inc=1, device_id=where, device_id_type=MESH)

    for dy, dx in PEERS:
        greet(place(ring(-1), peer(dy, dx), core))
    for dy, dx in PEERS[:-1]:
        greet(place(ctx, peer(dy, dx), core))
    for dy, dx in PEERS:
        greet(place(ctx, peer(dy, dx), 1 - core))
    greet(place(ring(1), head, core))
    pl.semaphore_wait(barrier, 3 * len(PEERS))

    ins = (q_ref, k_ref, v_ref)
    bufs = (q_buf, k_buf, v_buf)

    def columns(ref, t, where):
        return ref.at[:, pl.ds(pl.multiple_of(where * WIDTH[t], 128), WIDTH[t])]

    def landing(t, offset):
        return bufs[t].at[pl.ds(pl.multiple_of(offset + head * ROWS, ROWS), ROWS), :]

    def own_copy(t, n):
        to = peer(*PEERS[n])
        return pltpu.make_async_remote_copy(
            src_ref=columns(ins[t], t, to),
            dst_ref=landing(t, 0),
            send_sem=own_send.at[t, n],
            recv_sem=own_recv.at[t, n],
            device_id=place(ctx, to, core),
            device_id_type=MESH,
        )

    def far_copy(t, n):
        to = peer(*PEERS[n])
        return pltpu.make_async_remote_copy(
            src_ref=columns(ins[t], t, to),
            dst_ref=landing(t, BLK),
            send_sem=far_send.at[t - 1, n],
            recv_sem=far_recv.at[t - 1, n],
            device_id=place(ctx + 1, to, core),
            device_id_type=MESH,
        )

    def local_copy(t):
        return pltpu.make_async_copy(columns(ins[t], t, head), landing(t, 0), local_sem.at[t])

    def start_own(t):
        for n in range(7):
            own_copy(t, n).start()
        local_copy(t).start()

    def start_far(t):
        @pl.when(ctx < ctx_count - 1)
        def _():
            for n in range(8):
                far_copy(t, n).start()

    def wait_own(t):
        local_copy(t).wait()
        for n in range(7):
            own_copy(t, n).wait_recv()

    def wait_far(t):
        @pl.when(ctx > 0)
        def _():
            for n in range(8):
                far_copy(t, n).wait_recv()

    start_own(0)
    start_own(1)
    start_far(1)


    for n, step in enumerate(HEARD):
        for to in (ring(step), ring(-step)):
            pl.semaphore_signal(
                known_sem.at[n], inc=1, device_id=place(to, head, core), device_id_type=MESH
            )
        pl.semaphore_wait(known_sem.at[n], 2)

    ones_buf[...] = jnp.where(ctx > 0, 1.0, 0.0) * jnp.ones(ones_buf.shape, jnp.bfloat16)

    wait_own(0)
    wait_own(1)

    lanes = lax.broadcasted_iota(jnp.int32, (TILE, 2 * 128), 1)
    later = lax.broadcasted_iota(jnp.int32, (TILE, TILE), 0) < lax.broadcasted_iota(
        jnp.int32, (TILE, TILE), 1
    )
    contract = (((1,), (1,)), ((), ()))
    to_log2 = SCALE * math.log2(math.e)

    def head_window(h):
        return pl.ds(pl.multiple_of(h * 128, 128), 256)

    def head_query(h, rows):
        valid = (lanes >= DROPE * h) & (lanes < DQK + DROPE * h)
        return jnp.where(valid, q_buf[rows, head_window(h)], jnp.zeros((), jnp.bfloat16))

    @pl.loop(0, HEADS)
    def _(h):
        window = head_window(h)
        for i in range(BLK // TILE):
            rows = slice(i * TILE, (i + 1) * TILE)
            query = head_query(h, rows)
            diagonal = lax.dot_general(
                query, k_buf[rows, window], contract, preferred_element_type=jnp.float32
            )
            diagonal = jnp.where(later, -jnp.inf, diagonal)
            high = jnp.max(diagonal, axis=1, keepdims=True)
            if i > 0:
                before = lax.dot_general(
                    query, k_buf[: i * TILE, window], contract, preferred_element_type=jnp.float32
                )
                high = jnp.maximum(high, jnp.max(before, axis=1, keepdims=True))
                weights = jnp.exp2((before - high) * to_log2)
                p_buf[h, rows, : i * TILE] = weights.astype(jnp.bfloat16)
            weights = jnp.exp2((diagonal - high) * to_log2)
            p_buf[h, rows, rows] = weights.astype(jnp.bfloat16)
            high_buf[h, rows, :] = jnp.broadcast_to(high, (TILE, 128))

    wait_far(1)

    @pl.when(ctx == 0)
    def _():
        k_buf[BLK:, :] = jnp.broadcast_to(k_buf[0:1, :], (BLK, WIDTH[1]))

    @pl.loop(0, HEADS)
    def _(h):
        peak = jnp.full((1, 1), -jnp.inf, jnp.float32)
        for i in range(BLK // TILE):
            rows = slice(i * TILE, (i + 1) * TILE)
            scores = lax.dot_general(
                head_query(h, rows), k_buf[BLK:, head_window(h)], contract,
                preferred_element_type=jnp.float32,
            )
            far_buf[h, rows, :] = scores
            own_high = high_buf[h, rows, 0:1]
            high = jnp.maximum(own_high, jnp.max(scores, axis=1, keepdims=True))
            both_buf[h, rows, :] = jnp.broadcast_to(high, (TILE, 128))
            peak = jnp.maximum(peak, jnp.max(high, axis=0, keepdims=True))
        mine_buf[pl.ds(h, 1), :] = jnp.broadcast_to(peak * SCALE, (1, 128))

    def near_copy(step, dc):
        return pltpu.make_async_remote_copy(
            src_ref=mine_buf,
            dst_ref=near_buf.at[parity * GROUP + step],
            send_sem=near_send.at[step, dc],
            recv_sem=near_recv.at[parity * GROUP + step],
            device_id=place(
                group * GROUP + lax.rem(member + step, GROUP), target_head, lax.rem(core + dc, 2)
            ),
            device_id_type=MESH,
        )

    def near_arrival(par, step):
        return pltpu.make_async_remote_copy(
            src_ref=mine_buf,
            dst_ref=near_buf.at[par * GROUP + step],
            send_sem=near_send.at[step, 0],
            recv_sem=near_recv.at[par * GROUP + step],
            device_id=place(ctx, target_head, 1 - core),
            device_id_type=MESH,
        )

    for step in reversed(range(GROUP)):
        for dc in range(2):
            if step == 0 and dc == 0:

                @pl.when(jnp.logical_not(is_own_target))
                def _():
                    near_copy(0, 0).start()

                @pl.when(is_own_target)
                def _():
                    near_buf[pl.ds(parity * GROUP, 1)] = mine_buf[...][None]

            else:
                near_copy(step, dc).start()

    @pl.loop(0, HEADS)
    def _(h):
        for i in range(BLK // TILE):
            rows = slice(i * TILE, (i + 1) * TILE)
            own_high = high_buf[h, rows, 0:1]
            high = both_buf[h, rows, 0:1]
            weights = jnp.exp2((far_buf[h, rows, :] - high) * to_log2)
            p_buf[h, rows, BLK:] = weights.astype(jnp.bfloat16)
            high_buf[h, rows, :] = jnp.broadcast_to(
                jnp.exp2((own_high - high) * to_log2), (TILE, 128)
            )

    for par in range(2):

        @pl.when(jnp.logical_not((owner_base + par == head) & (owner_core == core)))
        def _():
            near_arrival(par, 0).wait_recv()

        for step in range(1, GROUP):
            near_arrival(par, step).wait_recv()
        part_buf[par] = jnp.max(near_buf[par * GROUP : (par + 1) * GROUP], axis=0)

    def wide_copy(step):
        return pltpu.make_async_remote_copy(
            src_ref=part_buf,
            dst_ref=wide_buf.at[step - 1],
            send_sem=wide_send.at[step - 1],
            recv_sem=wide_recv.at[step - 1],
            device_id=place(lax.rem(group + step, groups) * GROUP + member, head, core),
            device_id_type=MESH,
        )

    wide_order = sorted(range(1, groups), key=lambda step: -min(step, groups - step))
    for step in wide_order:
        wide_copy(step).start()

    start_own(2)
    start_far(2)

    def values(rows, h):
        return v_buf[rows, pl.ds(pl.multiple_of(h * 128, 128), DV)]

    wait_own(2)

    @pl.loop(0, HEADS)
    def _(h):
        for i in range(BLK // TILE):
            rows = slice(i * TILE, (i + 1) * TILE)
            own = slice(0, (i + 1) * TILE)
            right = jnp.concatenate(
                [values(own, h), jnp.ones(((i + 1) * TILE, 128), jnp.bfloat16)], axis=1
            )
            scale = high_buf[h, rows, :]
            acc_buf[h, rows, :] = jnp.concatenate([scale, scale], axis=1) * jnp.dot(
                p_buf[h, rows, own], right, preferred_element_type=jnp.float32
            )

    wait_far(2)

    @pl.when(ctx == 0)
    def _():
        v_buf[BLK:, :] = jnp.zeros((BLK, WIDTH[2]), jnp.bfloat16)

    @pl.loop(0, HEADS)
    def _(h):
        right = jnp.concatenate([values(slice(BLK, 2 * BLK), h), ones_buf[...]], axis=1)
        for i in range(BLK // TILE):
            rows = slice(i * TILE, (i + 1) * TILE)
            total = acc_buf[h, rows, :] + jnp.dot(
                p_buf[h, rows, BLK:], right, preferred_element_type=jnp.float32
            )
            out_ref[rows, pl.ds(pl.multiple_of(h * 128, 128), DV)] = (
                total[:, :DV] / total[:, DV:]
            ).astype(jnp.bfloat16)

    for step in wide_order:
        wide_copy(step).wait_recv()
    peak_ref[...] = jnp.maximum(part_buf[...], jnp.max(wide_buf[...], axis=0))

    for t in range(3):
        for n in range(7):
            own_copy(t, n).wait_send()

    @pl.when(ctx < ctx_count - 1)
    def _():
        for t in (1, 2):
            for n in range(8):
                far_copy(t, n).wait_send()

    for step in range(GROUP):
        for dc in range(2):
            if step == 0 and dc == 0:

                @pl.when(jnp.logical_not(is_own_target))
                def _():
                    near_copy(0, 0).wait_send()

            else:
                near_copy(step, dc).wait_send()
    for step in wide_order:
        wide_copy(step).wait_send()


def clip_kernel(att_ref, peak_ref, wq_ref, wk_ref, out_ref, cq_ref, ck_ref, hold, in_sem, out_sem):
    def inward(n):
        rows = pl.ds(n * TILE, TILE)
        return pltpu.make_async_copy(att_ref.at[rows, :], hold.at[rows, :], in_sem.at[n])

    def outward(n):
        rows = pl.ds(n * TILE, TILE)
        return pltpu.make_async_copy(hold.at[rows, :], out_ref.at[rows, :], out_sem.at[n])

    for n in range(BLK // TILE):
        inward(n).start()
    for n in range(BLK // TILE):
        inward(n).wait()
        outward(n).start()
    half = lax.broadcasted_iota(jnp.int32, (1, 128), 1) < DROPE
    for par in range(2):
        factors = jnp.minimum(1.0, CLIP / peak_ref[par])
        roots = jnp.sqrt(factors)
        first, second = factors[0:1], factors[1:2]
        root_first, root_second = roots[0:1], roots[1:2]
        tiles = (
            root_first,
            jnp.where(half, first, root_second),
            jnp.where(half, root_second, second),
        )
        for n, tile in enumerate(tiles):
            at = slice((par * 3 + n) * 128, (par * 3 + n + 1) * 128)
            cq_ref[:, at] = (wq_ref[:, at].astype(jnp.float32) * tile).astype(jnp.bfloat16)
        for n, tile in enumerate((root_first, root_second)):
            at = slice((par * 2 + n) * 128, (par * 2 + n + 1) * 128)
            ck_ref[:, at] = (wk_ref[:, at].astype(jnp.float32) * tile).astype(jnp.bfloat16)
    for n in range(BLK // TILE):
        outward(n).wait()


def body(query_rows, key_rows, value_rows, query_weight, key_weight):
    vmem = pl.BlockSpec(memory_space=pltpu.VMEM)
    hbm = pl.BlockSpec(memory_space=pl.ANY)
    groups = lax.axis_size("ctx") // GROUP
    dma = pltpu.SemaphoreType.DMA
    attended, peaks = pl.pallas_call(
        attention_kernel,
        out_shape=(
            jax.ShapeDtypeStruct((BLK, HEADS * DV), jnp.bfloat16),
            jax.ShapeDtypeStruct((2, HEADS, 128), jnp.float32),
        ),
        in_specs=[hbm, hbm, hbm],
        out_specs=(vmem, vmem),
        scratch_shapes=[
            pltpu.VMEM((BLK, WIDTH[0]), jnp.bfloat16),
            pltpu.VMEM((2 * BLK, WIDTH[1]), jnp.bfloat16),
            pltpu.VMEM((2 * BLK, WIDTH[2]), jnp.bfloat16),
            pltpu.VMEM((HEADS, BLK, 2 * BLK), jnp.bfloat16),
            pltpu.VMEM((HEADS, BLK, 2 * DV), jnp.float32),
            pltpu.VMEM((HEADS, BLK, 128), jnp.float32),
            pltpu.VMEM((HEADS, BLK, 128), jnp.float32),
            pltpu.VMEM((HEADS, BLK, BLK), jnp.float32),
            pltpu.VMEM((BLK, 128), jnp.bfloat16),
            pltpu.VMEM((HEADS, 128), jnp.float32),
            pltpu.VMEM((2 * GROUP, HEADS, 128), jnp.float32),
            pltpu.VMEM((2, HEADS, 128), jnp.float32),
            pltpu.VMEM((groups - 1, 2, HEADS, 128), jnp.float32),
            dma((3,)),
            dma((3, 7)),
            dma((3, 7)),
            dma((2, 8)),
            dma((2, 8)),
            dma((GROUP, 2)),
            dma((2 * GROUP,)),
            dma((groups - 1,)),
            dma((groups - 1,)),
            pltpu.SemaphoreType.REGULAR((len(HEARD),)),
        ],
        compiler_params=pltpu.CompilerParams(
            collective_id=0, has_side_effects=True, vmem_limit_bytes=56 * 1024 * 1024
        ),
        cost_estimate=pl.CostEstimate(
            flops=3_500_000_000, bytes_accessed=3_000_000, transcendentals=3_500_000
        ),
        name="attention",
    )(query_rows, key_rows, value_rows)
    return pl.pallas_call(
        clip_kernel,
        out_shape=(
            jax.ShapeDtypeStruct(attended.shape, jnp.bfloat16),
            jax.ShapeDtypeStruct(query_weight.shape, jnp.bfloat16),
            jax.ShapeDtypeStruct(key_weight.shape, jnp.bfloat16),
        ),
        in_specs=[hbm, vmem, vmem, vmem],
        out_specs=(hbm, vmem, vmem),
        scratch_shapes=[
            pltpu.VMEM(attended.shape, jnp.bfloat16),
            dma((BLK // TILE,)),
            dma((BLK // TILE,)),
        ],
        name="clip",
    )(attended, peaks, query_weight, key_weight)


def solution(mesh):
    rows = P(("ctx", "head"), "fsdp")
    weights = P(("ctx", "fsdp"), "head")
    return jax.shard_map(
        body,
        mesh=mesh,
        in_specs=(rows, rows, rows, weights, weights),
        out_specs=(P("ctx", ("fsdp", "head")), weights, weights),
        check_vma=False,
    )
```

```python
import functools
import math

import jax
import jax.numpy as jnp
from jax import lax
from jax.experimental import pallas as pl
from jax.experimental.pallas import tpu as pltpu
from jax.sharding import PartitionSpec as P

DNOPE = 128
DROPE = 64
DV = 128
DQK = 192
HEADS = 2
CLIP = 100.0
SCALE = DQK**-0.5
ROWS = 128
BLK = 1024
TILE = 256
GROUP = 4
HEARD = (1, 2, 4, 8, 16)
MESH = pl.DeviceIdType.MESH
WIDTH = (HEADS * DQK, HEADS * DQK, HEADS * DV)
PEERS = ((0, 1), (1, 0), (3, 0), (1, 1), (3, 1), (2, 0), (2, 1), (0, 0))


def attention_kernel(
    q_ref,
    k_ref,
    v_ref,
    out_ref,
    peak_ref,
    q_buf,
    k_buf,
    v_buf,
    p_buf,
    acc_buf,
    high_buf,
    s_buf,
    ones_buf,
    mine_buf,
    near_buf,
    part_buf,
    wide_buf,
    local_sem,
    own_send,
    own_recv,
    far_send,
    far_recv,
    near_send,
    near_recv,
    wide_send,
    wide_recv,
    known_sem,
):
    ctx = lax.axis_index("ctx")
    head = lax.axis_index("head")
    core = lax.axis_index("fsdp")
    ctx_count = lax.axis_size("ctx")
    y, x = head // 2, head % 2
    group, member = ctx // GROUP, ctx % GROUP
    groups = ctx_count // GROUP
    owner_core, owner_base = head // 4, 2 * (head % 4)
    target_head = 4 * core + head // 2
    parity = head % 2
    is_own_target = target_head == head

    def peer(dy, dx):
        return lax.rem(y + dy, 4) * 2 + lax.rem(x + dx, 2)

    def place(to_ctx, to_head, to_core):
        return {"ctx": to_ctx, "head": to_head, "fsdp": to_core}

    def ring(step):
        return lax.rem(ctx + step + ctx_count, ctx_count)

    barrier = pltpu.get_barrier_semaphore()

    def greet(where):
        pl.semaphore_signal(barrier, inc=1, device_id=where, device_id_type=MESH)

    for dy, dx in PEERS:
        greet(place(ring(-1), peer(dy, dx), core))
    for dy, dx in PEERS[:-1]:
        greet(place(ctx, peer(dy, dx), core))
    for dy, dx in PEERS:
        greet(place(ctx, peer(dy, dx), 1 - core))
    greet(place(ring(1), head, core))
    pl.semaphore_wait(barrier, 3 * len(PEERS))

    ins = (q_ref, k_ref, v_ref)
    bufs = (q_buf, k_buf, v_buf)

    def columns(ref, t, where):
        return ref.at[:, pl.ds(pl.multiple_of(where * WIDTH[t], 128), WIDTH[t])]

    def landing(t):
        return bufs[t].at[pl.ds(pl.multiple_of(head * ROWS, ROWS), ROWS), :]

    def own_copy(t, n):
        to = peer(*PEERS[n])
        return pltpu.make_async_remote_copy(
            src_ref=columns(ins[t], t, to),
            dst_ref=landing(t),
            send_sem=own_send.at[t, n],
            recv_sem=own_recv.at[t, n],
            device_id=place(ctx, to, core),
            device_id_type=MESH,
        )

    def far_copy(t, n):
        to = peer(*PEERS[n])
        return pltpu.make_async_remote_copy(
            src_ref=columns(ins[t], t, to),
            dst_ref=bufs[t].at[pl.ds(BLK + n * ROWS, ROWS), :],
            send_sem=far_send.at[t - 1, n],
            recv_sem=far_recv.at[t - 1, n],
            device_id=place(ctx + 1, to, core),
            device_id_type=MESH,
        )

    def local_copy(t):
        return pltpu.make_async_copy(columns(ins[t], t, head), landing(t), local_sem.at[t])

    def start(own, far):
        for n in range(7):
            for t in own:
                own_copy(t, n).start()

            @pl.when(ctx < ctx_count - 1)
            def _():
                far_copy(far, n).start()

        for t in own:
            local_copy(t).start()

        @pl.when(ctx < ctx_count - 1)
        def _():
            far_copy(far, 7).start()

    def wait_own(t):
        local_copy(t).wait()
        for n in range(7):
            own_copy(t, n).wait_recv()

    def wait_far(t, half):
        @pl.when(ctx > 0)
        def _():
            for n in range(4 * half, 4 * half + 4):
                far_copy(t, n).wait_recv()

    start((0, 1), 1)


    for n, step in enumerate(HEARD):
        for to in (ring(step), ring(-step)):
            pl.semaphore_signal(
                known_sem.at[n], inc=1, device_id=place(to, head, core), device_id_type=MESH
            )
        pl.semaphore_wait(known_sem.at[n], 2)

    ones_buf[...] = jnp.where(ctx > 0, 1.0, 0.0) * jnp.ones(ones_buf.shape, jnp.bfloat16)

    wait_own(0)
    wait_own(1)

    lanes = lax.broadcasted_iota(jnp.int32, (TILE, 2 * 128), 1)
    later = lax.broadcasted_iota(jnp.int32, (TILE, TILE), 0) < lax.broadcasted_iota(
        jnp.int32, (TILE, TILE), 1
    )
    contract = (((1,), (1,)), ((), ()))
    to_log2 = SCALE * math.log2(math.e)

    def head_window(h):
        return pl.ds(pl.multiple_of(h * 128, 128), 256)

    def head_query(h, rows):
        valid = (lanes >= DROPE * h) & (lanes < DQK + DROPE * h)
        return jnp.where(valid, q_buf[rows, head_window(h)], jnp.zeros((), jnp.bfloat16))

    def lane_max(part):
        return functools.reduce(
            jnp.maximum, [part[:, n : n + 128] for n in range(0, part.shape[1], 128)]
        )

    def head_scores(query, h, keys):
        return lax.dot_general(
            query, k_buf[keys, head_window(h)], contract, preferred_element_type=jnp.float32
        )

    @pl.loop(0, HEADS)
    def _(h):
        for i in range(BLK // TILE):
            rows = slice(i * TILE, (i + 1) * TILE)
            query = head_query(h, rows)
            diagonal = jnp.where(later, -jnp.inf, head_scores(query, h, rows))
            s_buf[h, rows, rows] = diagonal
            high = lane_max(diagonal)
            if i > 0:
                before = head_scores(query, h, slice(0, i * TILE))
                s_buf[h, rows, : i * TILE] = before
                high = jnp.maximum(high, lane_max(before))
            high_buf[h, rows, :] = high

    for half in range(2):
        wait_far(1, half)

        if half == 0:

            @pl.when(ctx == 0)
            def _():
                k_buf[BLK:, :] = jnp.broadcast_to(k_buf[0:1, :], (BLK, WIDTH[1]))

        keys = slice(BLK + half * (BLK // 2), BLK + (half + 1) * (BLK // 2))

        @pl.loop(0, HEADS)
        def _(h):
            top = jnp.full((TILE, 128), -jnp.inf, jnp.float32)
            for i in range(BLK // TILE):
                rows = slice(i * TILE, (i + 1) * TILE)
                scores = head_scores(head_query(h, rows), h, keys)
                s_buf[h, rows, keys] = scores
                high = jnp.maximum(high_buf[h, rows, :], lane_max(scores))
                high_buf[h, rows, :] = high
                top = jnp.maximum(top, high)
            if half == 1:
                peak = jnp.max(jnp.max(top, axis=0, keepdims=True), axis=1, keepdims=True)
                mine_buf[pl.ds(h, 1), :] = jnp.broadcast_to(peak * SCALE, (1, 128))

    def near_copy(step, dc):
        return pltpu.make_async_remote_copy(
            src_ref=mine_buf,
            dst_ref=near_buf.at[parity * GROUP + step],
            send_sem=near_send.at[step, dc],
            recv_sem=near_recv.at[parity * GROUP + step],
            device_id=place(
                group * GROUP + lax.rem(member + step, GROUP), target_head, lax.rem(core + dc, 2)
            ),
            device_id_type=MESH,
        )

    def near_arrival(par, step):
        return pltpu.make_async_remote_copy(
            src_ref=mine_buf,
            dst_ref=near_buf.at[par * GROUP + step],
            send_sem=near_send.at[step, 0],
            recv_sem=near_recv.at[par * GROUP + step],
            device_id=place(ctx, target_head, 1 - core),
            device_id_type=MESH,
        )

    for step in reversed(range(GROUP)):
        for dc in range(2):
            if step == 0 and dc == 0:

                @pl.when(jnp.logical_not(is_own_target))
                def _():
                    near_copy(0, 0).start()

                @pl.when(is_own_target)
                def _():
                    near_buf[pl.ds(parity * GROUP, 1)] = mine_buf[...][None]

            else:
                near_copy(step, dc).start()

    for par in range(2):

        @pl.when(jnp.logical_not((owner_base + par == head) & (owner_core == core)))
        def _():
            near_arrival(par, 0).wait_recv()

        for step in range(1, GROUP):
            near_arrival(par, step).wait_recv()
        part_buf[par] = jnp.max(near_buf[par * GROUP : (par + 1) * GROUP], axis=0)

    def wide_copy(step):
        return pltpu.make_async_remote_copy(
            src_ref=part_buf,
            dst_ref=wide_buf.at[step - 1],
            send_sem=wide_send.at[step - 1],
            recv_sem=wide_recv.at[step - 1],
            device_id=place(lax.rem(group + step, groups) * GROUP + member, head, core),
            device_id_type=MESH,
        )

    wide_order = sorted(range(1, groups), key=lambda step: -min(step, groups - step))
    for step in wide_order:
        wide_copy(step).start()

    start((2,), 2)

    @pl.loop(0, HEADS)
    def _(h):
        for i in range(BLK // TILE):
            rows = slice(i * TILE, (i + 1) * TILE)
            high = jnp.max(high_buf[h, rows, :], axis=1, keepdims=True)
            for keys in (slice(0, (i + 1) * TILE), slice(BLK, 2 * BLK)):
                weights = jnp.exp2((s_buf[h, rows, keys] - high) * to_log2)
                p_buf[h, rows, keys] = weights.astype(jnp.bfloat16)

    def values(rows, h):
        return v_buf[rows, pl.ds(pl.multiple_of(h * 128, 128), DV)]

    wait_own(2)

    @pl.loop(0, HEADS)
    def _(h):
        for i in range(BLK // TILE):
            rows = slice(i * TILE, (i + 1) * TILE)
            own = slice(0, (i + 1) * TILE)
            right = jnp.concatenate(
                [values(own, h), jnp.ones(((i + 1) * TILE, 128), jnp.bfloat16)], axis=1
            )
            acc_buf[h, rows, :] = jnp.dot(
                p_buf[h, rows, own], right, preferred_element_type=jnp.float32
            )

    wait_far(2, 0)
    wait_far(2, 1)

    @pl.when(ctx == 0)
    def _():
        v_buf[BLK:, :] = jnp.zeros((BLK, WIDTH[2]), jnp.bfloat16)

    @pl.loop(0, HEADS)
    def _(h):
        right = jnp.concatenate([values(slice(BLK, 2 * BLK), h), ones_buf[...]], axis=1)
        for i in range(BLK // TILE):
            rows = slice(i * TILE, (i + 1) * TILE)
            total = acc_buf[h, rows, :] + jnp.dot(
                p_buf[h, rows, BLK:], right, preferred_element_type=jnp.float32
            )
            out_ref[rows, pl.ds(pl.multiple_of(h * 128, 128), DV)] = (
                total[:, :DV] / total[:, DV:]
            ).astype(jnp.bfloat16)

    for step in wide_order:
        wide_copy(step).wait_recv()
    peak_ref[...] = jnp.maximum(part_buf[...], jnp.max(wide_buf[...], axis=0))

    for t in range(3):
        for n in range(7):
            own_copy(t, n).wait_send()

    @pl.when(ctx < ctx_count - 1)
    def _():
        for t in (1, 2):
            for n in range(8):
                far_copy(t, n).wait_send()

    for step in range(GROUP):
        for dc in range(2):
            if step == 0 and dc == 0:

                @pl.when(jnp.logical_not(is_own_target))
                def _():
                    near_copy(0, 0).wait_send()

            else:
                near_copy(step, dc).wait_send()
    for step in wide_order:
        wide_copy(step).wait_send()


def clip_kernel(att_ref, peak_ref, wq_ref, wk_ref, out_ref, cq_ref, ck_ref):
    out_ref[...] = att_ref[...]
    half = lax.broadcasted_iota(jnp.int32, (1, 128), 1) < DROPE
    for par in range(2):
        factors = jnp.minimum(1.0, CLIP / peak_ref[par])
        roots = jnp.sqrt(factors)
        first, second = factors[0:1], factors[1:2]
        root_first, root_second = roots[0:1], roots[1:2]
        tiles = (
            root_first,
            jnp.where(half, first, root_second),
            jnp.where(half, root_second, second),
        )
        for n, tile in enumerate(tiles):
            at = slice((par * 3 + n) * 128, (par * 3 + n + 1) * 128)
            cq_ref[:, at] = (wq_ref[:, at].astype(jnp.float32) * tile).astype(jnp.bfloat16)
        for n, tile in enumerate((root_first, root_second)):
            at = slice((par * 2 + n) * 128, (par * 2 + n + 1) * 128)
            ck_ref[:, at] = (wk_ref[:, at].astype(jnp.float32) * tile).astype(jnp.bfloat16)


def body(query_rows, key_rows, value_rows, query_weight, key_weight):
    vmem = pl.BlockSpec(memory_space=pltpu.VMEM)
    hbm = pl.BlockSpec(memory_space=pl.ANY)
    groups = lax.axis_size("ctx") // GROUP
    dma = pltpu.SemaphoreType.DMA
    attended, peaks = pl.pallas_call(
        attention_kernel,
        out_shape=(
            jax.ShapeDtypeStruct((BLK, HEADS * DV), jnp.bfloat16),
            jax.ShapeDtypeStruct((2, HEADS, 128), jnp.float32),
        ),
        in_specs=[hbm, hbm, hbm],
        out_specs=(vmem, vmem),
        scratch_shapes=[
            pltpu.VMEM((BLK, WIDTH[0]), jnp.bfloat16),
            pltpu.VMEM((2 * BLK, WIDTH[1]), jnp.bfloat16),
            pltpu.VMEM((2 * BLK, WIDTH[2]), jnp.bfloat16),
            pltpu.VMEM((HEADS, BLK, 2 * BLK), jnp.bfloat16),
            pltpu.VMEM((HEADS, BLK, 2 * DV), jnp.float32),
            pltpu.VMEM((HEADS, BLK, 128), jnp.float32),
            pltpu.VMEM((HEADS, BLK, 2 * BLK), jnp.float32),
            pltpu.VMEM((BLK, 128), jnp.bfloat16),
            pltpu.VMEM((HEADS, 128), jnp.float32),
            pltpu.VMEM((2 * GROUP, HEADS, 128), jnp.float32),
            pltpu.VMEM((2, HEADS, 128), jnp.float32),
            pltpu.VMEM((groups - 1, 2, HEADS, 128), jnp.float32),
            dma((3,)),
            dma((3, 7)),
            dma((3, 7)),
            dma((2, 8)),
            dma((2, 8)),
            dma((GROUP, 2)),
            dma((2 * GROUP,)),
            dma((groups - 1,)),
            dma((groups - 1,)),
            pltpu.SemaphoreType.REGULAR((len(HEARD),)),
        ],
        compiler_params=pltpu.CompilerParams(
            collective_id=0, has_side_effects=True, vmem_limit_bytes=56 * 1024 * 1024
        ),
        cost_estimate=pl.CostEstimate(
            flops=3_500_000_000, bytes_accessed=3_000_000, transcendentals=3_500_000
        ),
        name="attention",
    )(query_rows, key_rows, value_rows)
    return pl.pallas_call(
        clip_kernel,
        out_shape=(
            jax.ShapeDtypeStruct(attended.shape, jnp.bfloat16),
            jax.ShapeDtypeStruct(query_weight.shape, jnp.bfloat16),
            jax.ShapeDtypeStruct(key_weight.shape, jnp.bfloat16),
        ),
        in_specs=[vmem] * 4,
        out_specs=(vmem, vmem, vmem),
        name="clip",
    )(attended, peaks, query_weight, key_weight)


def solution(mesh):
    rows = P(("ctx", "head"), "fsdp")
    weights = P(("ctx", "fsdp"), "head")
    return jax.shard_map(
        body,
        mesh=mesh,
        in_specs=(rows, rows, rows, weights, weights),
        out_specs=(P("ctx", ("fsdp", "head")), weights, weights),
        check_vma=False,
    )
```

```python
import functools
import math

import jax
import jax.numpy as jnp
from jax import lax
from jax.experimental import pallas as pl
from jax.experimental.pallas import tpu as pltpu
from jax.sharding import PartitionSpec as P

DNOPE = 128
DROPE = 64
DV = 128
DQK = 192
HEADS = 2
CLIP = 100.0
SCALE = DQK**-0.5
ROWS = 128
PIECES = 2
PIECE = ROWS // PIECES
BLK = 1024
TILE = 256
GROUP = 4
HEARD = (1, 2, 4, 8, 16)
MESH = pl.DeviceIdType.MESH
WIDTH = (HEADS * DQK, HEADS * DQK, HEADS * DV)
PEERS = ((0, 1), (1, 0), (3, 0), (1, 1), (3, 1), (2, 0), (2, 1), (0, 0))


def attention_kernel(
    q_ref,
    k_ref,
    v_ref,
    out_ref,
    peak_ref,
    q_buf,
    k_buf,
    v_buf,
    p_buf,
    acc_buf,
    high_buf,
    s_buf,
    ones_buf,
    mine_buf,
    near_buf,
    part_buf,
    wide_buf,
    local_sem,
    own_send,
    own_recv,
    far_send,
    far_recv,
    near_send,
    near_recv,
    wide_send,
    wide_recv,
    known_sem,
):
    ctx = lax.axis_index("ctx")
    head = lax.axis_index("head")
    core = lax.axis_index("fsdp")
    ctx_count = lax.axis_size("ctx")
    y, x = head // 2, head % 2
    group, member = ctx // GROUP, ctx % GROUP
    groups = ctx_count // GROUP
    owner_core, owner_base = head // 4, 2 * (head % 4)
    target_head = 4 * core + head // 2
    parity = head % 2
    is_own_target = target_head == head

    def peer(dy, dx):
        return lax.rem(y + dy, 4) * 2 + lax.rem(x + dx, 2)

    def place(to_ctx, to_head, to_core):
        return {"ctx": to_ctx, "head": to_head, "fsdp": to_core}

    def ring(step):
        return lax.rem(ctx + step + ctx_count, ctx_count)

    barrier = pltpu.get_barrier_semaphore()

    def greet(where):
        pl.semaphore_signal(barrier, inc=1, device_id=where, device_id_type=MESH)

    for dy, dx in PEERS:
        greet(place(ring(-1), peer(dy, dx), core))
    for dy, dx in PEERS[:-1]:
        greet(place(ctx, peer(dy, dx), core))
    for dy, dx in PEERS:
        greet(place(ctx, peer(dy, dx), 1 - core))
    greet(place(ring(1), head, core))
    pl.semaphore_wait(barrier, 3 * len(PEERS))

    ins = (q_ref, k_ref, v_ref)
    bufs = (q_buf, k_buf, v_buf)

    def columns(ref, t, where, first=0, count=ROWS):
        return ref.at[pl.ds(first, count), pl.ds(pl.multiple_of(where * WIDTH[t], 128), WIDTH[t])]

    def landing(t, first=0, count=ROWS):
        return bufs[t].at[pl.ds(pl.multiple_of(head * ROWS + first, PIECE), count), :]

    def own_copy(t, n, piece):
        to = peer(*PEERS[n])
        return pltpu.make_async_remote_copy(
            src_ref=columns(ins[t], t, to, piece * PIECE, PIECE),
            dst_ref=landing(t, piece * PIECE, PIECE),
            send_sem=own_send.at[t, n, piece],
            recv_sem=own_recv.at[t, n, piece],
            device_id=place(ctx, to, core),
            device_id_type=MESH,
        )

    def far_copy(t, n, piece):
        to = peer(*PEERS[n])
        return pltpu.make_async_remote_copy(
            src_ref=columns(ins[t], t, to, piece * PIECE, PIECE),
            dst_ref=bufs[t].at[pl.ds(BLK + n * ROWS + piece * PIECE, PIECE), :],
            send_sem=far_send.at[t - 1, n, piece],
            recv_sem=far_recv.at[t - 1, n, piece],
            device_id=place(ctx + 1, to, core),
            device_id_type=MESH,
        )

    def local_copy(t):
        return pltpu.make_async_copy(columns(ins[t], t, head), landing(t), local_sem.at[t])

    def start(own, far):
        for n in range(7):
            for t in own:
                for piece in range(PIECES):
                    own_copy(t, n, piece).start()

            @pl.when(ctx < ctx_count - 1)
            def _():
                for piece in range(PIECES):
                    far_copy(far, n, piece).start()

        for t in own:
            local_copy(t).start()

        @pl.when(ctx < ctx_count - 1)
        def _():
            for piece in range(PIECES):
                far_copy(far, 7, piece).start()

    def wait_own(t):
        local_copy(t).wait()
        for n in range(7):
            for piece in range(PIECES):
                own_copy(t, n, piece).wait_recv()

    def wait_far(t, half):
        @pl.when(ctx > 0)
        def _():
            for n in range(4 * half, 4 * half + 4):
                for piece in range(PIECES):
                    far_copy(t, n, piece).wait_recv()

    start((0, 1), 1)


    for n, step in enumerate(HEARD):
        for to in (ring(step), ring(-step)):
            pl.semaphore_signal(
                known_sem.at[n], inc=1, device_id=place(to, head, core), device_id_type=MESH
            )
        pl.semaphore_wait(known_sem.at[n], 2)

    ones_buf[...] = jnp.where(ctx > 0, 1.0, 0.0) * jnp.ones(ones_buf.shape, jnp.bfloat16)

    wait_own(0)
    wait_own(1)

    lanes = lax.broadcasted_iota(jnp.int32, (TILE, 2 * 128), 1)
    later = lax.broadcasted_iota(jnp.int32, (TILE, TILE), 0) < lax.broadcasted_iota(
        jnp.int32, (TILE, TILE), 1
    )
    contract = (((1,), (1,)), ((), ()))
    to_log2 = SCALE * math.log2(math.e)

    def head_window(h):
        return pl.ds(pl.multiple_of(h * 128, 128), 256)

    def head_query(h, rows):
        valid = (lanes >= DROPE * h) & (lanes < DQK + DROPE * h)
        return jnp.where(valid, q_buf[rows, head_window(h)], jnp.zeros((), jnp.bfloat16))

    def lane_max(part):
        return functools.reduce(
            jnp.maximum, [part[:, n : n + 128] for n in range(0, part.shape[1], 128)]
        )

    def head_scores(query, h, keys):
        return lax.dot_general(
            query, k_buf[keys, head_window(h)], contract, preferred_element_type=jnp.float32
        )

    @pl.loop(0, HEADS)
    def _(h):
        for i in range(BLK // TILE):
            rows = slice(i * TILE, (i + 1) * TILE)
            query = head_query(h, rows)
            diagonal = jnp.where(later, -jnp.inf, head_scores(query, h, rows))
            s_buf[h, rows, rows] = diagonal
            high = lane_max(diagonal)
            if i > 0:
                before = head_scores(query, h, slice(0, i * TILE))
                s_buf[h, rows, : i * TILE] = before
                high = jnp.maximum(high, lane_max(before))
            high_buf[h, rows, :] = high

    for half in range(2):
        wait_far(1, half)

        if half == 0:

            @pl.when(ctx == 0)
            def _():
                k_buf[BLK:, :] = jnp.broadcast_to(k_buf[0:1, :], (BLK, WIDTH[1]))

        keys = slice(BLK + half * (BLK // 2), BLK + (half + 1) * (BLK // 2))

        @pl.loop(0, HEADS)
        def _(h):
            top = jnp.full((TILE, 128), -jnp.inf, jnp.float32)
            for i in range(BLK // TILE):
                rows = slice(i * TILE, (i + 1) * TILE)
                scores = head_scores(head_query(h, rows), h, keys)
                s_buf[h, rows, keys] = scores
                high = jnp.maximum(high_buf[h, rows, :], lane_max(scores))
                high_buf[h, rows, :] = high
                top = jnp.maximum(top, high)
            if half == 1:
                peak = jnp.max(jnp.max(top, axis=0, keepdims=True), axis=1, keepdims=True)
                mine_buf[pl.ds(h, 1), :] = jnp.broadcast_to(peak * SCALE, (1, 128))

    def near_copy(step, dc):
        return pltpu.make_async_remote_copy(
            src_ref=mine_buf,
            dst_ref=near_buf.at[parity * GROUP + step],
            send_sem=near_send.at[step, dc],
            recv_sem=near_recv.at[parity * GROUP + step],
            device_id=place(
                group * GROUP + lax.rem(member + step, GROUP), target_head, lax.rem(core + dc, 2)
            ),
            device_id_type=MESH,
        )

    def near_arrival(par, step):
        return pltpu.make_async_remote_copy(
            src_ref=mine_buf,
            dst_ref=near_buf.at[par * GROUP + step],
            send_sem=near_send.at[step, 0],
            recv_sem=near_recv.at[par * GROUP + step],
            device_id=place(ctx, target_head, 1 - core),
            device_id_type=MESH,
        )

    for step in reversed(range(GROUP)):
        for dc in range(2):
            if step == 0 and dc == 0:

                @pl.when(jnp.logical_not(is_own_target))
                def _():
                    near_copy(0, 0).start()

                @pl.when(is_own_target)
                def _():
                    near_buf[pl.ds(parity * GROUP, 1)] = mine_buf[...][None]

            else:
                near_copy(step, dc).start()

    for par in range(2):

        @pl.when(jnp.logical_not((owner_base + par == head) & (owner_core == core)))
        def _():
            near_arrival(par, 0).wait_recv()

        for step in range(1, GROUP):
            near_arrival(par, step).wait_recv()
        part_buf[par] = jnp.max(near_buf[par * GROUP : (par + 1) * GROUP], axis=0)

    def wide_copy(step):
        return pltpu.make_async_remote_copy(
            src_ref=part_buf,
            dst_ref=wide_buf.at[step - 1],
            send_sem=wide_send.at[step - 1],
            recv_sem=wide_recv.at[step - 1],
            device_id=place(lax.rem(group + step, groups) * GROUP + member, head, core),
            device_id_type=MESH,
        )

    wide_order = sorted(range(1, groups), key=lambda step: -min(step, groups - step))
    for step in wide_order:
        wide_copy(step).start()

    start((2,), 2)

    @pl.loop(0, HEADS)
    def _(h):
        for i in range(BLK // TILE):
            rows = slice(i * TILE, (i + 1) * TILE)
            high = jnp.max(high_buf[h, rows, :], axis=1, keepdims=True)
            for keys in (slice(0, (i + 1) * TILE), slice(BLK, 2 * BLK)):
                weights = jnp.exp2((s_buf[h, rows, keys] - high) * to_log2)
                p_buf[h, rows, keys] = weights.astype(jnp.bfloat16)

    def values(rows, h):
        return v_buf[rows, pl.ds(pl.multiple_of(h * 128, 128), DV)]

    wait_own(2)

    @pl.loop(0, HEADS)
    def _(h):
        for i in range(BLK // TILE):
            rows = slice(i * TILE, (i + 1) * TILE)
            own = slice(0, (i + 1) * TILE)
            right = jnp.concatenate(
                [values(own, h), jnp.ones(((i + 1) * TILE, 128), jnp.bfloat16)], axis=1
            )
            acc_buf[h, rows, :] = jnp.dot(
                p_buf[h, rows, own], right, preferred_element_type=jnp.float32
            )

    wait_far(2, 0)
    wait_far(2, 1)

    @pl.when(ctx == 0)
    def _():
        v_buf[BLK:, :] = jnp.zeros((BLK, WIDTH[2]), jnp.bfloat16)

    @pl.loop(0, HEADS)
    def _(h):
        right = jnp.concatenate([values(slice(BLK, 2 * BLK), h), ones_buf[...]], axis=1)
        for i in range(BLK // TILE):
            rows = slice(i * TILE, (i + 1) * TILE)
            total = acc_buf[h, rows, :] + jnp.dot(
                p_buf[h, rows, BLK:], right, preferred_element_type=jnp.float32
            )
            out_ref[rows, pl.ds(pl.multiple_of(h * 128, 128), DV)] = (
                total[:, :DV] / total[:, DV:]
            ).astype(jnp.bfloat16)

    for step in wide_order:
        wide_copy(step).wait_recv()
    peak_ref[...] = jnp.maximum(part_buf[...], jnp.max(wide_buf[...], axis=0))

    for t in range(3):
        for n in range(7):
            for piece in range(PIECES):
                own_copy(t, n, piece).wait_send()

    @pl.when(ctx < ctx_count - 1)
    def _():
        for t in (1, 2):
            for n in range(8):
                for piece in range(PIECES):
                    far_copy(t, n, piece).wait_send()

    for step in range(GROUP):
        for dc in range(2):
            if step == 0 and dc == 0:

                @pl.when(jnp.logical_not(is_own_target))
                def _():
                    near_copy(0, 0).wait_send()

            else:
                near_copy(step, dc).wait_send()
    for step in wide_order:
        wide_copy(step).wait_send()


def clip_kernel(att_ref, peak_ref, wq_ref, wk_ref, out_ref, cq_ref, ck_ref):
    out_ref[...] = att_ref[...]
    half = lax.broadcasted_iota(jnp.int32, (1, 128), 1) < DROPE
    for par in range(2):
        factors = jnp.minimum(1.0, CLIP / peak_ref[par])
        roots = jnp.sqrt(factors)
        first, second = factors[0:1], factors[1:2]
        root_first, root_second = roots[0:1], roots[1:2]
        tiles = (
            root_first,
            jnp.where(half, first, root_second),
            jnp.where(half, root_second, second),
        )
        for n, tile in enumerate(tiles):
            at = slice((par * 3 + n) * 128, (par * 3 + n + 1) * 128)
            cq_ref[:, at] = (wq_ref[:, at].astype(jnp.float32) * tile).astype(jnp.bfloat16)
        for n, tile in enumerate((root_first, root_second)):
            at = slice((par * 2 + n) * 128, (par * 2 + n + 1) * 128)
            ck_ref[:, at] = (wk_ref[:, at].astype(jnp.float32) * tile).astype(jnp.bfloat16)


def body(query_rows, key_rows, value_rows, query_weight, key_weight):
    vmem = pl.BlockSpec(memory_space=pltpu.VMEM)
    hbm = pl.BlockSpec(memory_space=pl.ANY)
    groups = lax.axis_size("ctx") // GROUP
    dma = pltpu.SemaphoreType.DMA
    attended, peaks = pl.pallas_call(
        attention_kernel,
        out_shape=(
            jax.ShapeDtypeStruct((BLK, HEADS * DV), jnp.bfloat16),
            jax.ShapeDtypeStruct((2, HEADS, 128), jnp.float32),
        ),
        in_specs=[hbm, hbm, hbm],
        out_specs=(vmem, vmem),
        scratch_shapes=[
            pltpu.VMEM((BLK, WIDTH[0]), jnp.bfloat16),
            pltpu.VMEM((2 * BLK, WIDTH[1]), jnp.bfloat16),
            pltpu.VMEM((2 * BLK, WIDTH[2]), jnp.bfloat16),
            pltpu.VMEM((HEADS, BLK, 2 * BLK), jnp.bfloat16),
            pltpu.VMEM((HEADS, BLK, 2 * DV), jnp.float32),
            pltpu.VMEM((HEADS, BLK, 128), jnp.float32),
            pltpu.VMEM((HEADS, BLK, 2 * BLK), jnp.float32),
            pltpu.VMEM((BLK, 128), jnp.bfloat16),
            pltpu.VMEM((HEADS, 128), jnp.float32),
            pltpu.VMEM((2 * GROUP, HEADS, 128), jnp.float32),
            pltpu.VMEM((2, HEADS, 128), jnp.float32),
            pltpu.VMEM((groups - 1, 2, HEADS, 128), jnp.float32),
            dma((3,)),
            dma((3, 7, PIECES)),
            dma((3, 7, PIECES)),
            dma((2, 8, PIECES)),
            dma((2, 8, PIECES)),
            dma((GROUP, 2)),
            dma((2 * GROUP,)),
            dma((groups - 1,)),
            dma((groups - 1,)),
            pltpu.SemaphoreType.REGULAR((len(HEARD),)),
        ],
        compiler_params=pltpu.CompilerParams(
            collective_id=0, has_side_effects=True, vmem_limit_bytes=56 * 1024 * 1024
        ),
        cost_estimate=pl.CostEstimate(
            flops=3_500_000_000, bytes_accessed=3_000_000, transcendentals=3_500_000
        ),
        name="attention",
    )(query_rows, key_rows, value_rows)
    return pl.pallas_call(
        clip_kernel,
        out_shape=(
            jax.ShapeDtypeStruct(attended.shape, jnp.bfloat16),
            jax.ShapeDtypeStruct(query_weight.shape, jnp.bfloat16),
            jax.ShapeDtypeStruct(key_weight.shape, jnp.bfloat16),
        ),
        in_specs=[vmem] * 4,
        out_specs=(vmem, vmem, vmem),
        name="clip",
    )(attended, peaks, query_weight, key_weight)


def solution(mesh):
    rows = P(("ctx", "head"), "fsdp")
    weights = P(("ctx", "fsdp"), "head")
    return jax.shard_map(
        body,
        mesh=mesh,
        in_specs=(rows, rows, rows, weights, weights),
        out_specs=(P("ctx", ("fsdp", "head")), weights, weights),
        check_vma=False,
    )
```
